32 devices in a mesh: groups: 2 (over x), rows: 8 (over z, y), shots: 2 (over core).
Axes of the slice: x: 2, y: 2, z: 4, core: 2. Of those that a mesh axis runs over, the one named last changes fastest.
Arguments:
- right_sides: bfloat16 [2, 16384, 512], P(None, 'rows', ('groups', 'shots')), parts along dimension 2, may hold values from -6 to 6
- panels: bfloat16 [2, 32768, 1024], P(None, ('groups', 'rows')), parts along dimension 1, may hold values from -0.125 to 0.125
- inverses: bfloat16 [8, 2, 256, 256], P('groups'), parts along dimension 0, may hold values from -0.25 to 0.25
- pivots: int32 [4], replicated, may hold values from 0 to 63, as said below
Outputs:
- regrouped: bfloat16 [2, 2, 256, 16384], P(None, 'shots', ('groups', 'rows')), parts along dimension 2
The draws below stay inside these ranges and needn't reach their ends.
There are 2 independent parts, one for each index of `groups`. The reference program is written for one: setup_inputs(seed, part) draws one part's arguments, and reference() takes and returns one part's arrays. A program takes and returns all parts, laid end to end along the dimension named above; an argument that names none is the same for every part. Nothing has to cross between parts.
Inputs may be any that keep to these rules, and one draw needn't show every extreme that they name: `pivots`: 4 distinct row block numbers.
All inputs are finite; a program needn't handle non-finite values.
Results may differ from the reference program's by a relative error of at most 0.0052.
Values may be sent and summed in bfloat16 or wider, within the bound.
No kernel may reach another device: no remote copies, remote signals or barrier semaphores. Data moves between devices by JAX's collectives and lax.ppermute only.
A program may use at most 64 MiB of HBM per device.

```python
import jax
import jax.numpy as jnp
from jax import lax

ORDER = 16384
PW = 256
PANELS = 4
SHOTS = 256
N_SHOTS = 2


def draw_pivots(key, part):
    key = jax.random.fold_in(key, 7)
    first_key, second_key = jax.random.split(key)
    blocks = ORDER // PW
    middle = jax.random.permutation(first_key, blocks - 2)[:PANELS - 2].astype(jnp.int32) + 1
    values = jnp.concatenate([jnp.zeros((1,), jnp.int32), middle, jnp.full((1,), blocks - 1, jnp.int32)])
    shuffle = jax.random.permutation(second_key, PANELS)
    return values[shuffle]


def shard_levels(key, dims, shards, smallest, high):
    factor_of = 1.0
    for position, shards_of in shards:
        draws = jax.random.uniform(jax.random.fold_in(jax.random.fold_in(key, 6), position), (shards_of,), jnp.float32, smallest / len(shards), high / len(shards))
        factor_of = factor_of * jnp.repeat(jnp.exp(draws), dims[position] // shards_of).reshape((-1,) + (1,) * (len(dims) - 1 - position))
    return factor_of


def gaussian(key, shape, spread, reach, shards=(), held_as=jnp.bfloat16):
    values = jax.random.normal(key, shape, jnp.float32) * spread
    if len(shards) > 0:
        values = shard_levels(key, shape, shards, -0.22, 0.18) * values
    return jnp.clip(values, min=-reach, max=reach).astype(held_as)


def setup_inputs(seed: int = 0, part: int = 0) -> dict:
    key_of = jax.random.split(jax.random.key(seed), 5)
    own_keys = jax.random.split(jax.random.fold_in(key_of[4], part), 5)
    return {
        "right_sides": gaussian(own_keys[0], (2, ORDER, SHOTS), 1.0, 6.0, ((1, 8), (2, 2))),
        "panels": gaussian(own_keys[1], (2, ORDER, PANELS * PW), (2 * PANELS * PW) ** -0.5, 0.125, ((1, 8),)),
        "inverses": gaussian(own_keys[2], (PANELS, 2, PW, PW), (2 * PW) ** -0.5, 0.25),
        "pivots": draw_pivots(jax.random.fold_in(key_of[4], 71), part),
    }


def complex_dot(matrix, vectors):
    real_part = jnp.dot(matrix[0], vectors[0], preferred_element_type=jnp.float32) - jnp.dot(matrix[1], vectors[1], preferred_element_type=jnp.float32)
    imag_part = jnp.dot(matrix[0], vectors[1], preferred_element_type=jnp.float32) + jnp.dot(matrix[1], vectors[0], preferred_element_type=jnp.float32)
    return jnp.stack([real_part, imag_part])


def reference(right_sides, panels, inverses, pivots):
    running = right_sides.astype(jnp.float32)
    row_slot = jnp.arange(ORDER, dtype=jnp.int32) // PW
    finished = jnp.zeros((ORDER,), dtype=jnp.bool_)
    for panel in range(PANELS):
        offset = (pivots[panel] * PW).astype(jnp.int32)
        pivot_rows = lax.dynamic_slice_in_dim(running, offset, PW, 1).astype(jnp.bfloat16)
        solved = complex_dot(inverses[panel], pivot_rows).astype(jnp.bfloat16)
        running = lax.dynamic_update_slice_in_dim(running, solved.astype(jnp.float32), offset, 1)
        finished = finished | (row_slot == pivots[panel])
        update = complex_dot(panels[:, :, panel * PW:(panel + 1) * PW], solved)
        running = jnp.where(finished[None, :, None], running, running - update)
    result = jnp.transpose(running.astype(jnp.bfloat16), (0, 2, 1))
    return result.reshape(2, N_SHOTS, SHOTS // N_SHOTS, ORDER)
```

```python
import functools

import jax
import jax.numpy as jnp
from jax import lax
from jax.experimental import pallas as pl
from jax.experimental.pallas import tpu as pltpu
from jax.sharding import PartitionSpec as P

CONTRACT_LAST = (((1,), (1,)), ((), ()))


def dot_t(left, right):
    return lax.dot_general(left, right, CONTRACT_LAST, preferred_element_type=jnp.float32)


def turned(vectors):
    half = vectors.shape[0] // 2
    return jnp.concatenate([-vectors[half:], vectors[:half]], axis=0)


def transposed_sides(sides):
    shots = sides.shape[2]
    row = lax.broadcasted_iota(jnp.int32, (shots, shots), 0)
    column = lax.broadcasted_iota(jnp.int32, (shots, shots), 1)
    unit = jnp.where(row == column, 1.0, 0.0).astype(jnp.bfloat16)
    return jnp.concatenate([dot_t(unit, sides[0]), dot_t(unit, sides[1])], axis=0)


def solve_kernel(count, slot_ref, sides_ref, inverse_ref, *refs):
    solved_refs, out_ref = refs[:-1], refs[-1]
    rows = transposed_sides(sides_ref)
    width = rows.shape[1]
    if count:
        panel_ref = solved_refs[0]
        for j in range(count):
            solved = solved_refs[1 + j][...]
            columns = slice(j * width, (j + 1) * width)
            rows = rows - dot_t(solved, panel_ref[0, :, columns])
            rows = rows - dot_t(turned(solved), panel_ref[1, :, columns])
    rows = rows.astype(jnp.bfloat16)
    solved = dot_t(rows, inverse_ref[0, 0]) + dot_t(turned(rows), inverse_ref[0, 1])
    out_ref[...] = solved.astype(jnp.bfloat16)


def solve(panel, slot, right_sides, panels, inverses, solved):
    parts, _, shots = right_sides.shape
    width = inverses.shape[-1]
    in_specs = [
        pl.BlockSpec((parts, width, shots), lambda i, s: (0, s[0], 0)),
        pl.BlockSpec((1, parts, width, width), lambda i, s: (panel, 0, 0, 0)),
    ]
    operands = [right_sides, inverses]
    if panel:
        in_specs.append(pl.BlockSpec((parts, width, panel * width), lambda i, s: (0, s[0], 0)))
        operands.append(panels)
    for block in solved:
        in_specs.append(pl.BlockSpec(block.shape, lambda i, s: (0, 0)))
        operands.append(block)
    return pl.pallas_call(
        functools.partial(solve_kernel, panel),
        out_shape=jax.ShapeDtypeStruct((parts * shots, width), jnp.bfloat16),
        grid_spec=pltpu.PrefetchScalarGridSpec(
            num_scalar_prefetch=1,
            grid=(1,),
            in_specs=in_specs,
            out_specs=pl.BlockSpec((parts * shots, width), lambda i, s: (0, 0)),
        ),
        compiler_params=pltpu.CompilerParams(vmem_limit_bytes=32 * 1024 * 1024),
        name="solve",
    )(slot, *operands)


def update_kernel(owners, place_ref, sides_ref, panel_ref, *refs):
    solved_refs, out_ref = refs[:-1], refs[-1]
    width = sides_ref.shape[1]
    block = place_ref[0] + pl.program_id(0)
    rows = transposed_sides(sides_ref)
    for j, solved_ref in enumerate(solved_refs):
        solved = solved_ref[...]
        columns = slice(j * width, (j + 1) * width)
        rows = rows - dot_t(solved, panel_ref[0, :, columns])
        rows = rows - dot_t(turned(solved), panel_ref[1, :, columns])
    shots = rows.shape[0] // 2
    each = shots // owners

    def write(values):
        for part in range(2):
            for owner in range(owners):
                start = part * shots + owner * each
                out_ref[owner, part] = values[start : start + each]

    write(rows.astype(jnp.bfloat16))
    for j, solved_ref in enumerate(solved_refs):

        @pl.when(place_ref[1 + j] == block)
        def _():
            write(solved_ref[...])


def update(place, right_sides, panels, solved, owners):
    parts, local_rows, shots = right_sides.shape
    width = solved[0].shape[1]
    each = shots // owners
    return pl.pallas_call(
        functools.partial(update_kernel, owners),
        out_shape=jax.ShapeDtypeStruct((owners, parts, each, local_rows), jnp.bfloat16),
        grid_spec=pltpu.PrefetchScalarGridSpec(
            num_scalar_prefetch=1,
            grid=(local_rows // width,),
            in_specs=[
                pl.BlockSpec((parts, width, shots), lambda i, s: (0, i, 0)),
                pl.BlockSpec((parts, width, panels.shape[2]), lambda i, s: (0, i, 0)),
            ]
            + [pl.BlockSpec(block.shape, lambda i, s: (0, 0)) for block in solved],
            out_specs=pl.BlockSpec((owners, parts, each, width), lambda i, s: (0, 0, 0, i)),
        ),
        compiler_params=pltpu.CompilerParams(vmem_limit_bytes=32 * 1024 * 1024),
        name="update",
    )(place, right_sides, panels, *solved)


def broadcast_any(block, owner):
    block = jnp.where(lax.axis_index("rows") == owner, block, jnp.zeros_like(block))
    return lax.psum(block, "rows")


def broadcast_pairs(block, owner, ranks):
    me = lax.axis_index("rows")
    lines = ranks // 2

    def branch(source):
        side = source % 2

        def run(value):
            have = jnp.where(me == source, value, jnp.zeros_like(value))
            for line in range(lines):
                if line != source // 2:
                    have = have + lax.ppermute(value, "rows", [(source, line * 2 + side)])
            across = [(line * 2 + side, line * 2 + 1 - side) for line in range(lines)]
            return jnp.where(me % 2 == side, have, lax.ppermute(have, "rows", across))

        return run

    return lax.switch(owner, [branch(source) for source in range(ranks)], block)


def body(ranks, right_sides, panels, inverses, pivots):
    me = lax.axis_index("rows")
    width = inverses.shape[-1]
    per_device = right_sides.shape[1] // width
    solved = []
    for panel in range(inverses.shape[0]):
        owner = pivots[panel] // per_device
        slot = (pivots[panel] % per_device).reshape(1)
        block = solve(panel, slot, right_sides, panels, inverses, solved)
        if ranks % 2 == 0 and ranks <= 8:
            solved.append(broadcast_pairs(block, owner, ranks))
        else:
            solved.append(broadcast_any(block, owner))
    place = jnp.concatenate([(me * per_device).reshape(1), pivots]).astype(jnp.int32)
    rows = update(place, right_sides, panels, solved, ranks)
    received = lax.all_to_all(rows, "rows", split_axis=0, concat_axis=0, tiled=True)
    regrouped = jnp.transpose(received, (1, 2, 0, 3))
    return regrouped.reshape(regrouped.shape[0], 1, regrouped.shape[1], -1)


def solution(mesh):
    placed = (
        P(None, "rows", ("groups", "shots")),
        P(None, ("groups", "rows"), None),
        P("groups", None, None, None),
        P(),
    )
    return jax.shard_map(
        functools.partial(body, mesh.shape["rows"]),
        mesh=mesh,
        in_specs=placed,
        out_specs=P(None, "shots", ("groups", "rows"), None),
        check_vma=False,
    )
```

```python
import functools

import jax
import jax.numpy as jnp
from jax import lax
from jax.experimental import pallas as pl
from jax.experimental.pallas import tpu as pltpu
from jax.sharding import PartitionSpec as P

CONTRACT_LAST = (((1,), (1,)), ((), ()))

BESIDE_PANELS = pltpu.CompilerParams(vmem_limit_bytes=57 * 1024 * 1024)
SMALL = pltpu.CompilerParams(vmem_limit_bytes=16 * 1024 * 1024)


def dot_t(left, right):
    return lax.dot_general(left, right, CONTRACT_LAST, preferred_element_type=jnp.float32)


def turned(vectors):
    half = vectors.shape[0] // 2
    return jnp.concatenate([-vectors[half:], vectors[:half]], axis=0)


def transposed_sides(sides):
    shots = sides.shape[2]
    row = lax.broadcasted_iota(jnp.int32, (shots, shots), 0)
    column = lax.broadcasted_iota(jnp.int32, (shots, shots), 1)
    unit = jnp.where(row == column, 1.0, 0.0).astype(jnp.bfloat16)
    return jnp.concatenate([dot_t(unit, sides[0]), dot_t(unit, sides[1])], axis=0)


def prepare_kernel(count, pivots_ref, inverse_ref, *refs):
    sides_refs, panel_refs, out_refs = refs[:count], refs[count : 2 * count - 1], refs[2 * count - 1 :]
    rows = transposed_sides(sides_refs[0]).astype(jnp.bfloat16)
    solved = dot_t(rows, inverse_ref[0, 0]) + dot_t(turned(rows), inverse_ref[0, 1])
    out_refs[0][...] = solved.astype(jnp.bfloat16)
    height, width = out_refs[0].shape
    for sides_ref, panel_ref, out_ref in zip(sides_refs[1:], panel_refs, out_refs[1:]):
        out_ref[:height] = transposed_sides(sides_ref).astype(jnp.bfloat16)
        pieces = [(j, p) for j in range(panel_ref.shape[2] // width) for p in range(panel_ref.shape[0])]
        for n, (j, p) in enumerate(pieces):
            out_ref[height + n * width : height + (n + 1) * width] = panel_ref[p, :, j * width : (j + 1) * width]


def prepare(pivots, right_sides, panels, inverses):
    parts, local_rows, shots = right_sides.shape
    count, width = inverses.shape[0], inverses.shape[-1]
    height = parts * shots
    per_device = local_rows // width

    def slot(panel):
        return lambda i, pivots_ref: (0, lax.rem(pivots_ref[panel], per_device), 0)

    shapes = [(height + parts * panel * width, width) for panel in range(count)]
    return pl.pallas_call(
        functools.partial(prepare_kernel, count),
        out_shape=[jax.ShapeDtypeStruct(shape, jnp.bfloat16) for shape in shapes],
        grid_spec=pltpu.PrefetchScalarGridSpec(
            num_scalar_prefetch=1,
            grid=(1,),
            in_specs=[pl.BlockSpec((1, parts, width, width), lambda i, *_: (0, 0, 0, 0))]
            + [pl.BlockSpec((parts, width, shots), slot(panel)) for panel in range(count)]
            + [pl.BlockSpec((parts, width, panel * width), slot(panel)) for panel in range(1, count)],
            out_specs=[pl.BlockSpec(shape, lambda i, *_: (0, 0)) for shape in shapes],
        ),
        compiler_params=BESIDE_PANELS,
        name="prepare",
    )(pivots, inverses, *[right_sides] * count, *[panels] * (count - 1))


def solve_kernel(own_ref, inverse_ref, *refs):
    solved_refs, out_ref = refs[:-1], refs[-1]
    height, width = out_ref.shape
    rows = own_ref[:height].astype(jnp.float32)
    for j, solved_ref in enumerate(solved_refs):
        solved = solved_ref[...]
        start = height + 2 * j * width
        rows = rows - dot_t(solved, own_ref[start : start + width])
        rows = rows - dot_t(turned(solved), own_ref[start + width : start + 2 * width])
    rows = rows.astype(jnp.bfloat16)
    solved = dot_t(rows, inverse_ref[0, 0]) + dot_t(turned(rows), inverse_ref[0, 1])
    out_ref[...] = solved.astype(jnp.bfloat16)


def solve(panel, own, inverses, solved):
    height, width = solved[0].shape
    return pl.pallas_call(
        solve_kernel,
        out_shape=jax.ShapeDtypeStruct((height, width), jnp.bfloat16),
        grid=(1,),
        in_specs=[
            pl.BlockSpec(own.shape, lambda i: (0, 0)),
            pl.BlockSpec((1,) + inverses.shape[1:], lambda i: (panel, 0, 0, 0)),
        ]
        + [pl.BlockSpec(block.shape, lambda i: (0, 0)) for block in solved],
        out_specs=pl.BlockSpec((height, width), lambda i: (0, 0)),
        compiler_params=SMALL,
        name="solve",
    )(own, inverses, *solved)


def update_kernel(owners, pivots_ref, first_ref, sides_ref, panel_ref, *refs):
    count = len(refs) - 3
    solved_refs, out_ref, real_ref, imag_ref = refs[:count], refs[-3], refs[-2], refs[-1]
    rows = sides_ref.shape[1]
    width = solved_refs[0].shape[1]

    @pl.when(pl.program_id(0) == 0)
    def _():
        for j, solved_ref in enumerate(solved_refs):
            solved = solved_ref[...]
            real_ref[:, j * width : (j + 1) * width] = solved
            imag_ref[:, j * width : (j + 1) * width] = turned(solved)

    values = transposed_sides(sides_ref) - dot_t(real_ref[...], panel_ref[0]) - dot_t(imag_ref[...], panel_ref[1])
    shots = values.shape[0] // 2
    each = shots // owners

    def write(block, columns):
        for part in range(2):
            for owner in range(owners):
                start = part * shots + owner * each
                out_ref[owner, part, :, columns] = block[start : start + each]

    write(values.astype(jnp.bfloat16), slice(None))
    first = first_ref[0] + pl.program_id(0) * (rows // width)
    for j, solved_ref in enumerate(solved_refs):
        for k in range(rows // width):

            @pl.when(pivots_ref[j] == first + k)
            def _():
                write(solved_ref[...], slice(k * width, (k + 1) * width))


def update(first, pivots, right_sides, panels, solved, owners):
    parts, local_rows, shots = right_sides.shape
    width = solved[0].shape[1]
    columns = panels.shape[2]
    each = shots // owners
    tile = 2 * width if local_rows % (2 * width) == 0 else width
    return pl.pallas_call(
        functools.partial(update_kernel, owners),
        out_shape=jax.ShapeDtypeStruct((owners, parts, each, local_rows), jnp.bfloat16),
        grid_spec=pltpu.PrefetchScalarGridSpec(
            num_scalar_prefetch=2,
            grid=(local_rows // tile,),
            in_specs=[
                pl.BlockSpec((parts, tile, shots), lambda i, *_: (0, i, 0)),
                pl.BlockSpec((parts, tile, columns), lambda i, *_: (0, i, 0)),
            ]
            + [pl.BlockSpec(block.shape, lambda i, *_: (0, 0)) for block in solved],
            out_specs=pl.BlockSpec((owners, parts, each, tile), lambda i, *_: (0, 0, 0, i)),
            scratch_shapes=[pltpu.VMEM((parts * shots, columns), jnp.bfloat16)] * 2,
        ),
        compiler_params=BESIDE_PANELS,
        name="update",
    )(pivots, first, right_sides, panels, *solved)


def regroup(received):
    owners, parts, shots, rows = received.shape
    return jnp.transpose(received, (1, 2, 0, 3)).reshape(parts, 1, shots, owners * rows)


def broadcast(block, owner, ranks):
    me = lax.axis_index("rows")

    def branch(source):
        line, side = source // 2, source % 2

        def at(hop, other):
            return (line ^ hop) * 2 + (side ^ other)

        def run(value):
            far = lax.ppermute(value, "rows", [(source, at(2, 0))])
            across = lax.ppermute(value, "rows", [(source, at(0, 1))])
            have = jnp.where(me == source, value, far + across)
            first = lax.ppermute(have, "rows", [(source, at(1, 0)), (at(2, 0), at(3, 0)), (at(0, 1), at(1, 1))])
            second = lax.ppermute(have, "rows", [(at(2, 0), at(2, 1)), (at(0, 1), at(3, 1))])
            return have + first + second

        return run

    return lax.switch(owner, [branch(source) for source in range(ranks)], block)


def solve_eight(owners, right_sides, panels, inverses, pivots):
    ranks = 8
    start, *own = prepare(pivots, right_sides, panels, inverses)
    solved = [broadcast(start, owners[0], ranks)]
    for panel in range(1, inverses.shape[0]):
        block = solve(panel, own[panel - 1], inverses, solved)
        solved.append(broadcast(block, owners[panel], ranks))
    return solved


def complex_dot(matrix, vectors):
    half = vectors.shape[0] // 2
    return dot_t(vectors, matrix[0]) + dot_t(turned(vectors), matrix[1])


def solve_summed(me, owners, right_sides, panels, inverses, pivots):
    parts, local_rows, shots = right_sides.shape
    width = inverses.shape[-1]
    solved = []
    for panel in range(inverses.shape[0]):
        offset = lax.rem(pivots[panel], local_rows // width) * width
        rows = lax.dynamic_slice_in_dim(right_sides, offset, width, 1)
        rows = jnp.transpose(rows, (0, 2, 1)).reshape(parts * shots, width).astype(jnp.float32)
        factor = lax.dynamic_slice_in_dim(panels, offset, width, 1)
        for j, block in enumerate(solved):
            rows = rows - complex_dot(factor[:, :, j * width : (j + 1) * width], block)
        block = complex_dot(inverses[panel], rows.astype(jnp.bfloat16)).astype(jnp.bfloat16)
        block = jnp.where(me == owners[panel], block, jnp.zeros_like(block))
        solved.append(lax.psum(block, "rows"))
    return solved


def body(ranks, right_sides, panels, inverses, pivots):
    me = lax.axis_index("rows")
    per_device = right_sides.shape[1] // inverses.shape[-1]
    owners = lax.div(pivots, jnp.full_like(pivots, per_device))
    if ranks == 8:
        solved = solve_eight(owners, right_sides, panels, inverses, pivots)
    else:
        solved = solve_summed(me, owners, right_sides, panels, inverses, pivots)
    first = (me * per_device).reshape(1)
    rows = update(first, pivots, right_sides, panels, solved, ranks)
    received = lax.all_to_all(rows, "rows", split_axis=0, concat_axis=0, tiled=True)
    return regroup(received)


def solution(mesh):
    placed = (
        P(None, "rows", ("groups", "shots")),
        P(None, ("groups", "rows"), None),
        P("groups", None, None, None),
        P(),
    )
    return jax.shard_map(
        functools.partial(body, mesh.shape["rows"]),
        mesh=mesh,
        in_specs=placed,
        out_specs=P(None, "shots", ("groups", "rows"), None),
        check_vma=False,
    )
```

```python
import functools

import jax
import jax.numpy as jnp
from jax import lax
from jax.experimental import pallas as pl
from jax.experimental.pallas import tpu as pltpu
from jax.sharding import PartitionSpec as P

CONTRACT_LAST = (((1,), (1,)), ((), ()))

BESIDE_PANELS = pltpu.CompilerParams(vmem_limit_bytes=57 * 1024 * 1024)
TILES = 4
SMALL = pltpu.CompilerParams(vmem_limit_bytes=16 * 1024 * 1024)


def dot_t(left, right):
    return lax.dot_general(left, right, CONTRACT_LAST, preferred_element_type=jnp.float32)


def turned(vectors):
    half = vectors.shape[0] // 2
    return jnp.concatenate([-vectors[half:], vectors[:half]], axis=0)


def transposed_sides(sides):
    shots = sides.shape[2]
    row = lax.broadcasted_iota(jnp.int32, (shots, shots), 0)
    column = lax.broadcasted_iota(jnp.int32, (shots, shots), 1)
    unit = jnp.where(row == column, 1.0, 0.0).astype(jnp.bfloat16)
    return jnp.concatenate([dot_t(unit, sides[0]), dot_t(unit, sides[1])], axis=0)


def first_kernel(per_device, pivots_ref, sides_ref, inverse_ref, out_ref, *owner_refs):
    for panel, owner_ref in enumerate(owner_refs):
        owner_ref[0] = lax.div(pivots_ref[panel], per_device)
    rows = transposed_sides(sides_ref).astype(jnp.bfloat16)
    solved = dot_t(rows, inverse_ref[0, 0]) + dot_t(turned(rows), inverse_ref[0, 1])
    out_ref[...] = solved.astype(jnp.bfloat16)


def solve_first(pivots, right_sides, inverses):
    parts, local_rows, shots = right_sides.shape
    count, width = inverses.shape[0], inverses.shape[-1]
    per_device = local_rows // width
    return pl.pallas_call(
        functools.partial(first_kernel, per_device),
        out_shape=[jax.ShapeDtypeStruct((parts * shots, width), jnp.bfloat16)]
        + [jax.ShapeDtypeStruct((1,), jnp.int32)] * count,
        grid_spec=pltpu.PrefetchScalarGridSpec(
            num_scalar_prefetch=1,
            grid=(1,),
            in_specs=[
                pl.BlockSpec((parts, width, shots), lambda i, p: (0, lax.rem(p[0], per_device), 0)),
                pl.BlockSpec((1, parts, width, width), lambda i, *_: (0, 0, 0, 0)),
            ],
            out_specs=[pl.BlockSpec((parts * shots, width), lambda i, *_: (0, 0))]
            + [pl.BlockSpec(memory_space=pltpu.SMEM)] * count,
        ),
        compiler_params=BESIDE_PANELS,
        name="solve_first",
    )(pivots, right_sides, inverses)


def prepare_kernel(count, pivots_ref, inverse_ref, *refs):
    sides_refs, panel_refs, out_refs = refs[: count - 1], refs[count - 1 : 2 * count - 2], refs[2 * count - 2 :]
    for panel, (sides_ref, panel_ref, out_ref) in enumerate(zip(sides_refs, panel_refs, out_refs), 1):
        parts, width, shots = sides_ref.shape
        for part in range(parts):
            out_ref[part * width : (part + 1) * width] = inverse_ref[panel, part]
        start = parts * width
        out_ref[start : start + parts * shots] = transposed_sides(sides_ref).astype(jnp.bfloat16)
        start += parts * shots
        pieces = [(j, p) for j in range(panel_ref.shape[2] // width) for p in range(parts)]
        for n, (j, p) in enumerate(pieces):
            out_ref[start + n * width : start + (n + 1) * width] = panel_ref[p, :, j * width : (j + 1) * width]


def prepare(pivots, right_sides, panels, inverses):
    parts, local_rows, shots = right_sides.shape
    count, width = inverses.shape[0], inverses.shape[-1]
    per_device = local_rows // width

    def slot(panel):
        return lambda i, pivots_ref: (0, lax.rem(pivots_ref[panel], per_device), 0)

    shapes = [(parts * (shots + (panel + 1) * width), width) for panel in range(1, count)]
    return pl.pallas_call(
        functools.partial(prepare_kernel, count),
        out_shape=[jax.ShapeDtypeStruct(shape, jnp.bfloat16) for shape in shapes],
        grid_spec=pltpu.PrefetchScalarGridSpec(
            num_scalar_prefetch=1,
            grid=(1,),
            in_specs=[pl.BlockSpec(inverses.shape, lambda i, *_: (0, 0, 0, 0))]
            + [pl.BlockSpec((parts, width, shots), slot(panel)) for panel in range(1, count)]
            + [pl.BlockSpec((parts, width, panel * width), slot(panel)) for panel in range(1, count)],
            out_specs=[pl.BlockSpec(shape, lambda i, *_: (0, 0)) for shape in shapes],
        ),
        compiler_params=BESIDE_PANELS,
        name="prepare",
    )(pivots, inverses, *[right_sides] * (count - 1), *[panels] * (count - 1))


def solve_kernel(own_ref, *refs):
    solved_refs, out_ref = refs[:-1], refs[-1]
    height, width = out_ref.shape
    start = 2 * width + height
    rows = own_ref[2 * width : start].astype(jnp.float32)
    for solved_ref in solved_refs:
        solved = solved_ref[...]
        rows = rows - dot_t(solved, own_ref[start : start + width])
        rows = rows - dot_t(turned(solved), own_ref[start + width : start + 2 * width])
        start += 2 * width
    rows = rows.astype(jnp.bfloat16)
    solved = dot_t(rows, own_ref[:width]) + dot_t(turned(rows), own_ref[width : 2 * width])
    out_ref[...] = solved.astype(jnp.bfloat16)


def solve(own, solved):
    height, width = solved[0].shape
    return pl.pallas_call(
        solve_kernel,
        out_shape=jax.ShapeDtypeStruct((height, width), jnp.bfloat16),
        grid=(1,),
        in_specs=[pl.BlockSpec(own.shape, lambda i: (0, 0))]
        + [pl.BlockSpec(block.shape, lambda i: (0, 0)) for block in solved],
        out_specs=pl.BlockSpec((height, width), lambda i: (0, 0)),
        compiler_params=SMALL,
        name="solve",
    )(own, *solved)


def early_kernel(sides_ref, panel_ref, *refs):
    solved_refs, (out_ref, real_ref, imag_ref) = refs[:-3], refs[-3:]
    width = solved_refs[0].shape[1]

    @pl.when(pl.program_id(0) == 0)
    def _():
        for j, solved_ref in enumerate(solved_refs):
            solved = solved_ref[...]
            real_ref[:, j * width : (j + 1) * width] = solved
            imag_ref[:, j * width : (j + 1) * width] = turned(solved)

    values = transposed_sides(sides_ref) - dot_t(real_ref[...], panel_ref[0])
    out_ref[...] = values - dot_t(imag_ref[...], panel_ref[1])


def early_update(right_sides, panels, solved):
    parts, local_rows, shots = right_sides.shape
    height, width = solved[0].shape
    columns = len(solved) * width
    tile = TILES * width if local_rows % (TILES * width) == 0 else width
    return pl.pallas_call(
        early_kernel,
        out_shape=jax.ShapeDtypeStruct((height, local_rows), jnp.float32),
        grid=(local_rows // tile,),
        in_specs=[
            pl.BlockSpec((parts, tile, shots), lambda i: (0, i, 0)),
            pl.BlockSpec((parts, tile, columns), lambda i: (0, i, 0)),
        ]
        + [pl.BlockSpec((height, width), lambda i: (0, 0)) for _ in solved],
        out_specs=pl.BlockSpec((height, tile), lambda i: (0, i)),
        scratch_shapes=[pltpu.VMEM((height, columns), jnp.bfloat16)] * 2,
        compiler_params=BESIDE_PANELS,
        name="early_update",
    )(right_sides, panels, *solved)


def last_kernel(owners, pivots_ref, first_ref, running_ref, panel_ref, *refs):
    solved_refs, out_ref = refs[:-1], refs[-1]
    rows = running_ref.shape[1]
    width = solved_refs[0].shape[1]
    solved = solved_refs[-1][...]
    values = running_ref[...] - dot_t(solved, panel_ref[0]) - dot_t(turned(solved), panel_ref[1])
    shots = values.shape[0] // 2
    each = shots // owners

    def write(block, columns):
        for part in range(2):
            for owner in range(owners):
                start = part * shots + owner * each
                out_ref[owner, part, :, columns] = block[start : start + each]

    write(values.astype(jnp.bfloat16), slice(None))
    first = first_ref[0] + pl.program_id(0) * (rows // width)
    for j, solved_ref in enumerate(solved_refs):
        for k in range(rows // width):

            @pl.when(pivots_ref[j] == first + k)
            def _():
                write(solved_ref[...], slice(k * width, (k + 1) * width))


def last_update(first, pivots, running, panels, solved, owners):
    parts, local_rows, columns = panels.shape
    height, width = solved[0].shape
    each = height // parts // owners
    tile = TILES * width if local_rows % (TILES * width) == 0 else width
    return pl.pallas_call(
        functools.partial(last_kernel, owners),
        out_shape=jax.ShapeDtypeStruct((owners, parts, each, local_rows), jnp.bfloat16),
        grid_spec=pltpu.PrefetchScalarGridSpec(
            num_scalar_prefetch=2,
            grid=(local_rows // tile,),
            in_specs=[
                pl.BlockSpec((height, tile), lambda i, *_: (0, i)),
                pl.BlockSpec((parts, tile, width), lambda i, *_: (0, i, columns // width - 1)),
            ]
            + [pl.BlockSpec(block.shape, lambda i, *_: (0, 0)) for block in solved],
            out_specs=pl.BlockSpec((owners, parts, each, tile), lambda i, *_: (0, 0, 0, i)),
        ),
        compiler_params=BESIDE_PANELS,
        name="last_update",
    )(pivots, first, running, panels, *solved)


def regroup_kernel(rows_ref, out_ref, sems):
    owners, _, _, rows = rows_ref.shape
    copies = [
        pltpu.make_async_copy(rows_ref.at[owner], out_ref.at[:, 0, :, pl.ds(owner * rows, rows)], sems.at[owner])
        for owner in range(owners)
    ]
    for copy in copies:
        copy.start()
    for copy in copies:
        copy.wait()


def regroup(received):
    owners, parts, shots, rows = received.shape
    return pl.pallas_call(
        regroup_kernel,
        out_shape=jax.ShapeDtypeStruct((parts, 1, shots, owners * rows), received.dtype),
        in_specs=[pl.BlockSpec(memory_space=pltpu.VMEM)],
        out_specs=pl.BlockSpec(memory_space=pl.ANY),
        scratch_shapes=[pltpu.SemaphoreType.DMA((owners,))],
        compiler_params=SMALL,
        name="regroup",
    )(received)


TREES = (
    ((4, 3), ((0, 1), (4, 7), (3, 5)), ((0, 2), (4, 6))),
    ((5, 2), ((1, 0), (5, 6), (2, 4)), ((1, 3), (5, 7))),
    ((3, 4), ((2, 0), (3, 7), (4, 5)), ((2, 6), (3, 1))),
    ((2, 5), ((3, 1), (2, 6), (5, 4)), ((3, 7), (2, 0))),
    ((5, 2), ((4, 0), (5, 1), (2, 3)), ((4, 6), (5, 7))),
    ((4, 3), ((5, 1), (4, 0), (3, 2)), ((5, 7), (4, 6))),
    ((2, 5), ((6, 4), (2, 1), (5, 3)), ((6, 7), (2, 0))),
    ((3, 4), ((7, 5), (3, 0), (4, 2)), ((7, 6), (3, 1))),
)


def broadcast(block, owner, beside):
    me = lax.axis_index("rows")

    def send(value, *pairs):
        return lax.ppermute(value, "rows", pairs)

    def branch(source):
        (one, two), first, second = TREES[source]

        def run(value):
            have = send(value, (source, one)) + send(value, (source, two))
            have = jnp.where(me == source, value, have)
            results = beside()
            return have + send(have, *first) + send(have, *second), results

        return run

    return lax.switch(owner, [branch(source) for source in range(len(TREES))], block)


def solve_eight(first, right_sides, panels, inverses, pivots):
    last = inverses.shape[0] - 1
    block, *owners = solve_first(pivots, right_sides, inverses)
    owners = [owner[0] for owner in owners]
    block, own = broadcast(block, owners[0], lambda: prepare(pivots, right_sides, panels, inverses))
    solved = [block]
    for panel in range(1, last):
        block = solve(own[panel - 1], solved)
        solved.append(broadcast(block, owners[panel], lambda: ())[0])
    block = solve(own[last - 1], solved)
    block, running = broadcast(block, owners[last], lambda: early_update(right_sides, panels, solved))
    solved.append(block)
    return last_update(first, pivots, running, panels, solved, len(TREES))


def complex_dot(matrix, vectors):
    half = vectors.shape[0] // 2
    return dot_t(vectors, matrix[0]) + dot_t(turned(vectors), matrix[1])


def solve_summed(me, owners, right_sides, panels, inverses, pivots):
    parts, local_rows, shots = right_sides.shape
    width = inverses.shape[-1]
    solved = []
    for panel in range(inverses.shape[0]):
        offset = lax.rem(pivots[panel], local_rows // width) * width
        rows = lax.dynamic_slice_in_dim(right_sides, offset, width, 1)
        rows = jnp.transpose(rows, (0, 2, 1)).reshape(parts * shots, width).astype(jnp.float32)
        factor = lax.dynamic_slice_in_dim(panels, offset, width, 1)
        for j, block in enumerate(solved):
            rows = rows - complex_dot(factor[:, :, j * width : (j + 1) * width], block)
        block = complex_dot(inverses[panel], rows.astype(jnp.bfloat16)).astype(jnp.bfloat16)
        block = jnp.where(me == owners[panel], block, jnp.zeros_like(block))
        solved.append(lax.psum(block, "rows"))
    return solved


def body(ranks, right_sides, panels, inverses, pivots):
    me = lax.axis_index("rows")
    per_device = right_sides.shape[1] // inverses.shape[-1]
    first = (me * per_device).reshape(1)
    if ranks == len(TREES):
        rows = solve_eight(first, right_sides, panels, inverses, pivots)
    else:
        owners = lax.div(pivots, jnp.full_like(pivots, per_device))
        solved = solve_summed(me, owners, right_sides, panels, inverses, pivots)
        running = early_update(right_sides, panels, solved[:-1])
        rows = last_update(first, pivots, running, panels, solved, ranks)
    received = lax.all_to_all(rows, "rows", split_axis=0, concat_axis=0, tiled=True)
    return regroup(received)


def solution(mesh):
    placed = (
        P(None, "rows", ("groups", "shots")),
        P(None, ("groups", "rows"), None),
        P("groups", None, None, None),
        P(),
    )
    return jax.shard_map(
        functools.partial(body, mesh.shape["rows"]),
        mesh=mesh,
        in_specs=placed,
        out_specs=P(None, "shots", ("groups", "rows"), None),
        check_vma=False,
    )
```

```python
import functools

import jax
import jax.numpy as jnp
from jax import lax
from jax.experimental import pallas as pl
from jax.experimental.pallas import tpu as pltpu
from jax.sharding import PartitionSpec as P

CONTRACT_LAST = (((1,), (1,)), ((), ()))

BESIDE_PANELS = pltpu.CompilerParams(vmem_limit_bytes=40 * 1024 * 1024)
TILES = 4
RANKS = 8
SMALL = pltpu.CompilerParams(vmem_limit_bytes=16 * 1024 * 1024)


def dot_t(left, right):
    return lax.dot_general(left, right, CONTRACT_LAST, preferred_element_type=jnp.float32)


def turned(vectors):
    half = vectors.shape[0] // 2
    return jnp.concatenate([-vectors[half:], vectors[:half]], axis=0)


def transposed_sides(sides):
    shots = sides.shape[2]
    row = lax.broadcasted_iota(jnp.int32, (shots, shots), 0)
    column = lax.broadcasted_iota(jnp.int32, (shots, shots), 1)
    unit = jnp.where(row == column, 1.0, 0.0).astype(jnp.bfloat16)
    return jnp.concatenate([dot_t(unit, sides[0]), dot_t(unit, sides[1])], axis=0)


def first_kernel(per_device, pivots_ref, sides_ref, inverse_ref, out_ref, *owner_refs):
    for panel, owner_ref in enumerate(owner_refs):
        owner_ref[0] = lax.div(pivots_ref[panel], per_device)
    rows = transposed_sides(sides_ref).astype(jnp.bfloat16)
    solved = dot_t(rows, inverse_ref[0, 0]) + dot_t(turned(rows), inverse_ref[0, 1])
    out_ref[...] = solved.astype(jnp.bfloat16)


def solve_first(pivots, right_sides, inverses):
    parts, local_rows, shots = right_sides.shape
    count, width = inverses.shape[0], inverses.shape[-1]
    per_device = local_rows // width
    return pl.pallas_call(
        functools.partial(first_kernel, per_device),
        out_shape=[jax.ShapeDtypeStruct((parts * shots, width), jnp.bfloat16)]
        + [jax.ShapeDtypeStruct((1,), jnp.int32)] * count,
        grid_spec=pltpu.PrefetchScalarGridSpec(
            num_scalar_prefetch=1,
            grid=(1,),
            in_specs=[
                pl.BlockSpec((parts, width, shots), lambda i, p: (0, lax.rem(p[0], per_device), 0)),
                pl.BlockSpec((1, parts, width, width), lambda i, *_: (0, 0, 0, 0)),
            ],
            out_specs=[pl.BlockSpec((parts * shots, width), lambda i, *_: (0, 0))]
            + [pl.BlockSpec(memory_space=pltpu.SMEM)] * count,
        ),
        compiler_params=BESIDE_PANELS,
        name="solve_first",
    )(pivots, right_sides, inverses)


def prepare_kernel(panels, pivots_ref, inverse_ref, *refs):
    count = len(panels)
    sides_refs, panel_refs, out_refs = refs[:count], refs[count : 2 * count], refs[2 * count :]
    for panel, sides_ref, panel_ref, out_ref in zip(panels, sides_refs, panel_refs, out_refs):
        parts, width, shots = sides_ref.shape
        for part in range(parts):
            out_ref[part * width : (part + 1) * width] = inverse_ref[panel, part]
        start = parts * width
        out_ref[start : start + parts * shots] = transposed_sides(sides_ref).astype(jnp.bfloat16)
        start += parts * shots
        pieces = [(j, p) for j in range(panel_ref.shape[2] // width) for p in range(parts)]
        for n, (j, p) in enumerate(pieces):
            out_ref[start + n * width : start + (n + 1) * width] = panel_ref[p, :, j * width : (j + 1) * width]


def prepare(numbers, pivots, right_sides, panels, inverses):
    parts, local_rows, shots = right_sides.shape
    width = inverses.shape[-1]
    per_device = local_rows // width

    def slot(panel):
        return lambda i, pivots_ref: (0, lax.rem(pivots_ref[panel], per_device), 0)

    shapes = [(parts * (shots + (panel + 1) * width), width) for panel in numbers]
    return pl.pallas_call(
        functools.partial(prepare_kernel, numbers),
        out_shape=[jax.ShapeDtypeStruct(shape, jnp.bfloat16) for shape in shapes],
        grid_spec=pltpu.PrefetchScalarGridSpec(
            num_scalar_prefetch=1,
            grid=(1,),
            in_specs=[pl.BlockSpec(inverses.shape, lambda i, *_: (0, 0, 0, 0))]
            + [pl.BlockSpec((parts, width, shots), slot(panel)) for panel in numbers]
            + [pl.BlockSpec((parts, width, panel * width), slot(panel)) for panel in numbers],
            out_specs=[pl.BlockSpec(shape, lambda i, *_: (0, 0)) for shape in shapes],
        ),
        compiler_params=BESIDE_PANELS,
        name="prepare",
    )(pivots, inverses, *[right_sides] * len(numbers), *[panels] * len(numbers))


def solve_kernel(own_ref, *refs):
    solved_refs, out_ref = refs[:-1], refs[-1]
    height, width = out_ref.shape
    start = 2 * width + height
    rows = own_ref[2 * width : start].astype(jnp.float32)
    for solved_ref in solved_refs:
        solved = solved_ref[...]
        rows = rows - dot_t(solved, own_ref[start : start + width])
        rows = rows - dot_t(turned(solved), own_ref[start + width : start + 2 * width])
        start += 2 * width
    rows = rows.astype(jnp.bfloat16)
    solved = dot_t(rows, own_ref[:width]) + dot_t(turned(rows), own_ref[width : 2 * width])
    out_ref[...] = solved.astype(jnp.bfloat16)


def solve(own, solved):
    height, width = solved[0].shape
    return pl.pallas_call(
        solve_kernel,
        out_shape=jax.ShapeDtypeStruct((height, width), jnp.bfloat16),
        grid=(1,),
        in_specs=[pl.BlockSpec(own.shape, lambda i: (0, 0))]
        + [pl.BlockSpec(block.shape, lambda i: (0, 0)) for block in solved],
        out_specs=pl.BlockSpec((height, width), lambda i: (0, 0)),
        compiler_params=SMALL,
        name="solve",
    )(own, *solved)


def early_kernel(sides_ref, panel_ref, *refs):
    solved_refs, (out_ref, panel_out_ref, real_ref, imag_ref) = refs[:-4], refs[-4:]
    width = solved_refs[0].shape[1]

    @pl.when(pl.program_id(0) == 0)
    def _():
        for j, solved_ref in enumerate(solved_refs):
            solved = solved_ref[...]
            real_ref[:, j * width : (j + 1) * width] = solved
            imag_ref[:, j * width : (j + 1) * width] = turned(solved)

    columns = len(solved_refs) * width
    panel_out_ref[...] = panel_ref[:, :, columns:]
    values = transposed_sides(sides_ref) - dot_t(real_ref[...], panel_ref[0, :, :columns])
    out_ref[...] = values - dot_t(imag_ref[...], panel_ref[1, :, :columns])


def early_update(right_sides, panels, solved):
    parts, local_rows, shots = right_sides.shape
    height, width = solved[0].shape
    columns = len(solved) * width
    rest = panels.shape[2] - columns
    tile = TILES * width if local_rows % (TILES * width) == 0 else width
    return pl.pallas_call(
        early_kernel,
        out_shape=[
            jax.ShapeDtypeStruct((height, local_rows), jnp.float32),
            jax.ShapeDtypeStruct((parts, local_rows, rest), jnp.bfloat16),
        ],
        grid=(local_rows // tile,),
        in_specs=[
            pl.BlockSpec((parts, tile, shots), lambda i: (0, i, 0)),
            pl.BlockSpec((parts, tile, panels.shape[2]), lambda i: (0, i, 0)),
        ]
        + [pl.BlockSpec((height, width), lambda i: (0, 0)) for _ in solved],
        out_specs=[
            pl.BlockSpec((height, tile), lambda i: (0, i)),
            pl.BlockSpec((parts, tile, rest), lambda i: (0, i, 0)),
        ],
        scratch_shapes=[pltpu.VMEM((height, columns), jnp.bfloat16)] * 2,
        compiler_params=BESIDE_PANELS,
        name="early_update",
    )(right_sides, panels, *solved)


def last_kernel(owners, pivots_ref, first_ref, running_ref, panel_ref, *refs):
    solved_refs, out_ref = refs[:-1], refs[-1]
    height, rows = running_ref.shape
    width = solved_refs[0].shape[1]
    shots = height // 2
    each = shots // owners

    def write(values, k):
        for part in range(2):
            for owner in range(owners):
                start = part * shots + owner * each
                out_ref[owner, part, :, k * width : (k + 1) * width] = values[start : start + each]

    solved = solved_refs[-1][...]
    around = turned(solved)
    for k in range(rows // width):
        columns = slice(k * width, (k + 1) * width)
        values = running_ref[:, columns] - dot_t(solved, panel_ref[0, columns])
        write((values - dot_t(around, panel_ref[1, columns])).astype(jnp.bfloat16), k)
        for j, solved_ref in enumerate(solved_refs):

            @pl.when(pivots_ref[j] == first_ref[0] + k)
            def _():
                write(solved_ref[...], k)


def last_update(first, pivots, running, panel, solved, owners):
    parts, local_rows, _ = panel.shape
    height, width = solved[0].shape
    each = height // parts // owners
    return pl.pallas_call(
        functools.partial(last_kernel, owners),
        out_shape=jax.ShapeDtypeStruct((owners, parts, each, local_rows), jnp.bfloat16),
        in_specs=[pl.BlockSpec(memory_space=pltpu.SMEM)] * 2
        + [pl.BlockSpec(memory_space=pltpu.VMEM)] * (2 + len(solved)),
        out_specs=pl.BlockSpec(memory_space=pltpu.VMEM),
        compiler_params=SMALL,
        name="last_update",
    )(pivots, first, running, panel, *solved)


def regroup_kernel(rows_ref, out_ref, sems):
    owners, _, _, rows = rows_ref.shape
    copies = [
        pltpu.make_async_copy(rows_ref.at[owner], out_ref.at[:, 0, :, pl.ds(owner * rows, rows)], sems.at[owner])
        for owner in range(owners)
    ]
    for copy in copies:
        copy.start()
    for copy in copies:
        copy.wait()


def regroup(received):
    owners, parts, shots, rows = received.shape
    return pl.pallas_call(
        regroup_kernel,
        out_shape=jax.ShapeDtypeStruct((parts, 1, shots, owners * rows), received.dtype),
        in_specs=[pl.BlockSpec(memory_space=pltpu.VMEM)],
        out_specs=pl.BlockSpec(memory_space=pl.ANY),
        scratch_shapes=[pltpu.SemaphoreType.DMA((owners,))],
        compiler_params=SMALL,
        name="regroup",
    )(received)


def broadcast(block, owner, beside):
    me = lax.axis_index("rows")

    def branch(source):
        def run(value):
            early = [lax.ppermute(value, "rows", [(source, source ^ step)]) for step in (4, 1)]
            have = jnp.where(me == source, value, early[0] + early[1])
            results = beside()
            corner = [source ^ step for step in (0, 1, 4, 5)]
            third = lax.ppermute(have, "rows", sorted((device, device ^ 2) for device in corner))
            fourth = lax.ppermute(have, "rows", [(source ^ 4, source ^ 5), (source, source ^ 7)])
            return have + third + fourth, results

        return run

    return lax.switch(owner, [branch(source) for source in range(RANKS)], block)


def solve_eight(first, right_sides, panels, inverses, pivots):
    last = inverses.shape[0] - 1
    block, *owners = solve_first(pivots, right_sides, inverses)
    owners = [owner[0] for owner in owners]
    block, own = broadcast(block, owners[0], lambda: prepare((1,), pivots, right_sides, panels, inverses))
    solved = [block]
    for panel in range(1, last):
        block = solve(own[-1], solved)
        block, more = broadcast(
            block, owners[panel], lambda: prepare((panel + 1,), pivots, right_sides, panels, inverses)
        )
        own = own + more
        solved.append(block)
    block = solve(own[last - 1], solved)
    block, (running, panel) = broadcast(block, owners[last], lambda: early_update(right_sides, panels, solved))
    solved.append(block)
    return last_update(first, pivots, running, panel, solved, RANKS)


def complex_dot(matrix, vectors):
    half = vectors.shape[0] // 2
    return dot_t(vectors, matrix[0]) + dot_t(turned(vectors), matrix[1])


def solve_summed(me, owners, right_sides, panels, inverses, pivots):
    parts, local_rows, shots = right_sides.shape
    width = inverses.shape[-1]
    solved = []
    for panel in range(inverses.shape[0]):
        offset = lax.rem(pivots[panel], local_rows // width) * width
        rows = lax.dynamic_slice_in_dim(right_sides, offset, width, 1)
        rows = jnp.transpose(rows, (0, 2, 1)).reshape(parts * shots, width).astype(jnp.float32)
        factor = lax.dynamic_slice_in_dim(panels, offset, width, 1)
        for j, block in enumerate(solved):
            rows = rows - complex_dot(factor[:, :, j * width : (j + 1) * width], block)
        block = complex_dot(inverses[panel], rows.astype(jnp.bfloat16)).astype(jnp.bfloat16)
        block = jnp.where(me == owners[panel], block, jnp.zeros_like(block))
        solved.append(lax.psum(block, "rows"))
    return solved


def body(ranks, right_sides, panels, inverses, pivots):
    me = lax.axis_index("rows")
    per_device = right_sides.shape[1] // inverses.shape[-1]
    first = (me * per_device).reshape(1)
    if ranks == RANKS:
        rows = solve_eight(first, right_sides, panels, inverses, pivots)
    else:
        owners = lax.div(pivots, jnp.full_like(pivots, per_device))
        solved = solve_summed(me, owners, right_sides, panels, inverses, pivots)
        running, panel = early_update(right_sides, panels, solved[:-1])
        rows = last_update(first, pivots, running, panel, solved, ranks)
    received = lax.all_to_all(rows, "rows", split_axis=0, concat_axis=0, tiled=True)
    return regroup(received)


def solution(mesh):
    placed = (
        P(None, "rows", ("groups", "shots")),
        P(None, ("groups", "rows"), None),
        P("groups", None, None, None),
        P(),
    )
    return jax.shard_map(
        functools.partial(body, mesh.shape["rows"]),
        mesh=mesh,
        in_specs=placed,
        out_specs=P(None, "shots", ("groups", "rows"), None),
        check_vma=False,
    )
```

```python
import functools

import jax
import jax.numpy as jnp
from jax import lax
from jax.experimental import pallas as pl
from jax.experimental.pallas import tpu as pltpu
from jax.sharding import PartitionSpec as P

CONTRACT_LAST = (((1,), (1,)), ((), ()))

BESIDE_PANELS = pltpu.CompilerParams(vmem_limit_bytes=40 * 1024 * 1024)
TILES = 4
RANKS = 8
SMALL = pltpu.CompilerParams(vmem_limit_bytes=16 * 1024 * 1024)


def dot_t(left, right):
    return lax.dot_general(left, right, CONTRACT_LAST, preferred_element_type=jnp.float32)


def turned(vectors):
    half = vectors.shape[0] // 2
    return jnp.concatenate([-vectors[half:], vectors[:half]], axis=0)


def transposed_sides(sides):
    shots = sides.shape[2]
    row = lax.broadcasted_iota(jnp.int32, (shots, shots), 0)
    column = lax.broadcasted_iota(jnp.int32, (shots, shots), 1)
    unit = jnp.where(row == column, 1.0, 0.0).astype(jnp.bfloat16)
    return jnp.concatenate([dot_t(unit, sides[0]), dot_t(unit, sides[1])], axis=0)


def first_kernel(per_device, pivots_ref, sides_ref, inverse_ref, out_ref, *owner_refs):
    for panel, owner_ref in enumerate(owner_refs):
        owner_ref[0] = lax.div(pivots_ref[panel], per_device)
    rows = transposed_sides(sides_ref).astype(jnp.bfloat16)
    solved = dot_t(rows, inverse_ref[0, 0]) + dot_t(turned(rows), inverse_ref[0, 1])
    out_ref[...] = solved.astype(jnp.bfloat16)


def solve_first(pivots, right_sides, inverses):
    parts, local_rows, shots = right_sides.shape
    count, width = inverses.shape[0], inverses.shape[-1]
    per_device = local_rows // width
    return pl.pallas_call(
        functools.partial(first_kernel, per_device),
        out_shape=[jax.ShapeDtypeStruct((parts * shots, width), jnp.bfloat16)]
        + [jax.ShapeDtypeStruct((1,), jnp.int32)] * count,
        grid_spec=pltpu.PrefetchScalarGridSpec(
            num_scalar_prefetch=1,
            grid=(1,),
            in_specs=[
                pl.BlockSpec((parts, width, shots), lambda i, p: (0, lax.rem(p[0], per_device), 0)),
                pl.BlockSpec((1, parts, width, width), lambda i, *_: (0, 0, 0, 0)),
            ],
            out_specs=[pl.BlockSpec((parts * shots, width), lambda i, *_: (0, 0))]
            + [pl.BlockSpec(memory_space=pltpu.SMEM)] * count,
        ),
        compiler_params=BESIDE_PANELS,
        name="solve_first",
    )(pivots, right_sides, inverses)


def prepare_kernel(panels, pivots_ref, inverse_ref, *refs):
    count = len(panels)
    sides_refs, panel_refs, out_refs = refs[:count], refs[count : 2 * count], refs[2 * count :]
    for panel, sides_ref, panel_ref, out_ref in zip(panels, sides_refs, panel_refs, out_refs):
        parts, width, shots = sides_ref.shape
        for part in range(parts):
            out_ref[part * width : (part + 1) * width] = inverse_ref[panel, part]
        start = parts * width
        out_ref[start : start + parts * shots] = transposed_sides(sides_ref).astype(jnp.bfloat16)
        start += parts * shots
        pieces = [(j, p) for j in range(panel_ref.shape[2] // width) for p in range(parts)]
        for n, (j, p) in enumerate(pieces):
            out_ref[start + n * width : start + (n + 1) * width] = panel_ref[p, :, j * width : (j + 1) * width]


def prepare(numbers, pivots, right_sides, panels, inverses):
    parts, local_rows, shots = right_sides.shape
    width = inverses.shape[-1]
    per_device = local_rows // width

    def slot(panel):
        return lambda i, pivots_ref: (0, lax.rem(pivots_ref[panel], per_device), 0)

    shapes = [(parts * (shots + (panel + 1) * width), width) for panel in numbers]
    return pl.pallas_call(
        functools.partial(prepare_kernel, numbers),
        out_shape=[jax.ShapeDtypeStruct(shape, jnp.bfloat16) for shape in shapes],
        grid_spec=pltpu.PrefetchScalarGridSpec(
            num_scalar_prefetch=1,
            grid=(1,),
            in_specs=[pl.BlockSpec(inverses.shape, lambda i, *_: (0, 0, 0, 0))]
            + [pl.BlockSpec((parts, width, shots), slot(panel)) for panel in numbers]
            + [pl.BlockSpec((parts, width, panel * width), slot(panel)) for panel in numbers],
            out_specs=[pl.BlockSpec(shape, lambda i, *_: (0, 0)) for shape in shapes],
        ),
        compiler_params=BESIDE_PANELS,
        name="prepare",
    )(pivots, inverses, *[right_sides] * len(numbers), *[panels] * len(numbers))


def solve_kernel(own_ref, *refs):
    solved_refs, out_ref = refs[:-1], refs[-1]
    height, width = out_ref.shape
    start = 2 * width + height
    rows = own_ref[2 * width : start].astype(jnp.float32)
    for solved_ref in solved_refs:
        solved = solved_ref[...]
        rows = rows - dot_t(solved, own_ref[start : start + width])
        rows = rows - dot_t(turned(solved), own_ref[start + width : start + 2 * width])
        start += 2 * width
    rows = rows.astype(jnp.bfloat16)
    solved = dot_t(rows, own_ref[:width]) + dot_t(turned(rows), own_ref[width : 2 * width])
    out_ref[...] = solved.astype(jnp.bfloat16)


def solve(own, solved):
    height, width = solved[0].shape
    return pl.pallas_call(
        solve_kernel,
        out_shape=jax.ShapeDtypeStruct((height, width), jnp.bfloat16),
        grid=(1,),
        in_specs=[pl.BlockSpec(own.shape, lambda i: (0, 0))]
        + [pl.BlockSpec(block.shape, lambda i: (0, 0)) for block in solved],
        out_specs=pl.BlockSpec((height, width), lambda i: (0, 0)),
        compiler_params=SMALL,
        name="solve",
    )(own, *solved)


def early_kernel(sides_ref, panel_ref, *refs):
    solved_refs, (out_ref, panel_out_ref, real_ref, imag_ref) = refs[:-4], refs[-4:]
    width = solved_refs[0].shape[1]

    @pl.when(pl.program_id(0) == 0)
    def _():
        for j, solved_ref in enumerate(solved_refs):
            solved = solved_ref[...]
            real_ref[:, j * width : (j + 1) * width] = solved
            imag_ref[:, j * width : (j + 1) * width] = turned(solved)

    columns = len(solved_refs) * width
    panel_out_ref[...] = panel_ref[:, :, columns:]
    values = transposed_sides(sides_ref) - dot_t(real_ref[...], panel_ref[0, :, :columns])
    out_ref[...] = values - dot_t(imag_ref[...], panel_ref[1, :, :columns])


def early_update(right_sides, panels, solved):
    parts, local_rows, shots = right_sides.shape
    height, width = solved[0].shape
    columns = len(solved) * width
    rest = panels.shape[2] - columns
    tile = TILES * width if local_rows % (TILES * width) == 0 else width
    return pl.pallas_call(
        early_kernel,
        out_shape=[
            jax.ShapeDtypeStruct((height, local_rows), jnp.float32),
            jax.ShapeDtypeStruct((parts, local_rows, rest), jnp.bfloat16),
        ],
        grid=(local_rows // tile,),
        in_specs=[
            pl.BlockSpec((parts, tile, shots), lambda i: (0, i, 0)),
            pl.BlockSpec((parts, tile, panels.shape[2]), lambda i: (0, i, 0)),
        ]
        + [pl.BlockSpec((height, width), lambda i: (0, 0)) for _ in solved],
        out_specs=[
            pl.BlockSpec((height, tile), lambda i: (0, i)),
            pl.BlockSpec((parts, tile, rest), lambda i: (0, i, 0)),
        ],
        scratch_shapes=[pltpu.VMEM((height, columns), jnp.bfloat16)] * 2,
        compiler_params=BESIDE_PANELS,
        name="early_update",
    )(right_sides, panels, *solved)


def last_kernel(panels, pivots_ref, me_ref, running_ref, panel_ref, *refs):
    width = panel_ref.shape[2]
    height, rows = running_ref.shape
    solved_refs, out_refs, whole_ref = refs[:panels], refs[panels:-1], refs[-1]
    count = len(out_refs)
    solved = solved_refs[-1][...]
    around = turned(solved)
    first = me_ref[0] * (rows // width)
    for k in range(rows // width):
        columns = slice(k * width, (k + 1) * width)
        values = running_ref[:, columns] - dot_t(solved, panel_ref[0, columns])
        whole_ref[:, columns] = (values - dot_t(around, panel_ref[1, columns])).astype(jnp.bfloat16)
    for j, solved_ref in enumerate(solved_refs):
        for k in range(rows // width):

            @pl.when(pivots_ref[j] == first + k)
            def _():
                whole_ref[:, k * width : (k + 1) * width] = solved_ref[...]

    each = height // 2 // count
    for step, out_ref in enumerate(out_refs):
        for part in range(2):
            start = pl.multiple_of((part * count + (me_ref[0] ^ step)) * each, each)
            out_ref[part] = whole_ref[pl.ds(start, each), :]


def last_update(me, pivots, running, panel, solved, owners):
    parts, local_rows, _ = panel.shape
    height, width = solved[0].shape
    each = height // parts // owners
    return pl.pallas_call(
        functools.partial(last_kernel, len(solved)),
        out_shape=[jax.ShapeDtypeStruct((parts, each, local_rows), jnp.bfloat16)] * owners,
        in_specs=[pl.BlockSpec(memory_space=pltpu.SMEM)] * 2
        + [pl.BlockSpec(memory_space=pltpu.VMEM)] * (2 + len(solved)),
        out_specs=[pl.BlockSpec(memory_space=pltpu.VMEM)] * owners,
        scratch_shapes=[pltpu.VMEM((height, local_rows), jnp.bfloat16)],
        compiler_params=SMALL,
        name="last_update",
    )(pivots, me, running, panel, *solved)


def regroup_kernel(me_ref, *refs):
    block_refs, out_ref, sems = refs[:-2], refs[-2], refs[-1]
    rows = block_refs[0].shape[2]
    copies = []
    for step, block_ref in enumerate(block_refs):
        start = pl.multiple_of((me_ref[0] ^ step) * rows, rows)
        copies.append(pltpu.make_async_copy(block_ref, out_ref.at[:, 0, :, pl.ds(start, rows)], sems.at[step]))
    for copy in copies:
        copy.start()
    for copy in copies:
        copy.wait()


def regroup(me, blocks):
    parts, shots, rows = blocks[0].shape
    return pl.pallas_call(
        regroup_kernel,
        out_shape=jax.ShapeDtypeStruct((parts, 1, shots, len(blocks) * rows), blocks[0].dtype),
        grid_spec=pltpu.PrefetchScalarGridSpec(
            num_scalar_prefetch=1,
            grid=(1,),
            in_specs=[pl.BlockSpec(memory_space=pltpu.VMEM)] * len(blocks),
            out_specs=pl.BlockSpec(memory_space=pl.ANY),
            scratch_shapes=[pltpu.SemaphoreType.DMA((len(blocks),))],
        ),
        compiler_params=SMALL,
        name="regroup",
    )(me, *blocks)


def broadcast(block, owner, beside):
    me = lax.axis_index("rows")

    def branch(source):
        def run(value):
            early = [lax.ppermute(value, "rows", [(source, source ^ step)]) for step in (1, 4)]
            have = jnp.where(me == source, value, early[0] + early[1])
            results = beside()
            corner = [source ^ step for step in (0, 1, 4, 5)]
            fourth = lax.ppermute(have, "rows", [(source ^ 4, source ^ 5), (source, source ^ 7)])
            third = lax.ppermute(have, "rows", sorted((device, device ^ 2) for device in corner))
            return have + third + fourth, results

        return run

    return lax.switch(owner, [branch(source) for source in range(RANKS)], block)


def solve_eight(right_sides, panels, inverses, pivots):
    last = inverses.shape[0] - 1
    block, *owners = solve_first(pivots, right_sides, inverses)
    owners = [owner[0] for owner in owners]
    block, own = broadcast(block, owners[0], lambda: prepare((1,), pivots, right_sides, panels, inverses))
    solved = [block]
    for panel in range(1, last):
        block = solve(own[-1], solved)
        block, more = broadcast(
            block, owners[panel], lambda: prepare((panel + 1,), pivots, right_sides, panels, inverses)
        )
        own = own + more
        solved.append(block)
    block = solve(own[last - 1], solved)
    block, (running, panel) = broadcast(block, owners[last], lambda: early_update(right_sides, panels, solved))
    solved.append(block)
    return solved, running, panel


def complex_dot(matrix, vectors):
    half = vectors.shape[0] // 2
    return dot_t(vectors, matrix[0]) + dot_t(turned(vectors), matrix[1])


def solve_summed(me, owners, right_sides, panels, inverses, pivots):
    parts, local_rows, shots = right_sides.shape
    width = inverses.shape[-1]
    solved = []
    for panel in range(inverses.shape[0]):
        offset = lax.rem(pivots[panel], local_rows // width) * width
        rows = lax.dynamic_slice_in_dim(right_sides, offset, width, 1)
        rows = jnp.transpose(rows, (0, 2, 1)).reshape(parts * shots, width).astype(jnp.float32)
        factor = lax.dynamic_slice_in_dim(panels, offset, width, 1)
        for j, block in enumerate(solved):
            rows = rows - complex_dot(factor[:, :, j * width : (j + 1) * width], block)
        block = complex_dot(inverses[panel], rows.astype(jnp.bfloat16)).astype(jnp.bfloat16)
        block = jnp.where(me == owners[panel], block, jnp.zeros_like(block))
        solved.append(lax.psum(block, "rows"))
    return solved


def body(ranks, right_sides, panels, inverses, pivots):
    me = lax.axis_index("rows")
    if ranks == RANKS:
        solved, running, panel = solve_eight(right_sides, panels, inverses, pivots)
    else:
        per_device = right_sides.shape[1] // inverses.shape[-1]
        owners = lax.div(pivots, jnp.full_like(pivots, per_device))
        solved = solve_summed(me, owners, right_sides, panels, inverses, pivots)
        running, panel = early_update(right_sides, panels, solved[:-1])
    me = me.reshape(1)
    blocks = list(last_update(me, pivots, running, panel, solved, ranks))
    for step in range(1, ranks):
        blocks[step] = lax.ppermute(blocks[step], "rows", [(i, i ^ step) for i in range(ranks)])
    return regroup(me, blocks)


def solution(mesh):
    placed = (
        P(None, "rows", ("groups", "shots")),
        P(None, ("groups", "rows"), None),
        P("groups", None, None, None),
        P(),
    )
    return jax.shard_map(
        functools.partial(body, mesh.shape["rows"]),
        mesh=mesh,
        in_specs=placed,
        out_specs=P(None, "shots", ("groups", "rows"), None),
        check_vma=False,
    )
```

```python
import functools

import jax
import jax.numpy as jnp
from jax import lax
from jax.experimental import pallas as pl
from jax.experimental.pallas import tpu as pltpu
from jax.sharding import PartitionSpec as P

CONTRACT_LAST = (((1,), (1,)), ((), ()))

BESIDE_PANELS = pltpu.CompilerParams(vmem_limit_bytes=40 * 1024 * 1024)
TILES = 4
RANKS = 8
SMALL = pltpu.CompilerParams(vmem_limit_bytes=16 * 1024 * 1024)


def dot_t(left, right):
    return lax.dot_general(left, right, CONTRACT_LAST, preferred_element_type=jnp.float32)


def turned(vectors):
    half = vectors.shape[0] // 2
    return jnp.concatenate([-vectors[half:], vectors[:half]], axis=0)


def transposed_sides(sides):
    shots = sides.shape[2]
    row = lax.broadcasted_iota(jnp.int32, (shots, shots), 0)
    column = lax.broadcasted_iota(jnp.int32, (shots, shots), 1)
    unit = jnp.where(row == column, 1.0, 0.0).astype(jnp.bfloat16)
    return jnp.concatenate([dot_t(unit, sides[0]), dot_t(unit, sides[1])], axis=0)


def first_kernel(per_device, pivots_ref, sides_ref, inverse_ref, out_ref, *owner_refs):
    for panel, owner_ref in enumerate(owner_refs):
        owner_ref[0] = lax.div(pivots_ref[panel], per_device)
    rows = transposed_sides(sides_ref).astype(jnp.bfloat16)
    solved = dot_t(rows, inverse_ref[0, 0]) + dot_t(turned(rows), inverse_ref[0, 1])
    out_ref[...] = solved.astype(jnp.bfloat16)


def solve_first(pivots, right_sides, inverses):
    parts, local_rows, shots = right_sides.shape
    count, width = inverses.shape[0], inverses.shape[-1]
    per_device = local_rows // width
    return pl.pallas_call(
        functools.partial(first_kernel, per_device),
        out_shape=[jax.ShapeDtypeStruct((parts * shots, width), jnp.bfloat16)]
        + [jax.ShapeDtypeStruct((1,), jnp.int32)] * count,
        grid_spec=pltpu.PrefetchScalarGridSpec(
            num_scalar_prefetch=1,
            grid=(1,),
            in_specs=[
                pl.BlockSpec((parts, width, shots), lambda i, p: (0, lax.rem(p[0], per_device), 0)),
                pl.BlockSpec((1, parts, width, width), lambda i, *_: (0, 0, 0, 0)),
            ],
            out_specs=[pl.BlockSpec((parts * shots, width), lambda i, *_: (0, 0))]
            + [pl.BlockSpec(memory_space=pltpu.SMEM)] * count,
        ),
        compiler_params=BESIDE_PANELS,
        name="solve_first",
    )(pivots, right_sides, inverses)


def prepare_kernel(panels, pivots_ref, inverse_ref, *refs):
    count = len(panels)
    sides_refs, panel_refs, out_refs = refs[:count], refs[count : 2 * count], refs[2 * count :]
    for panel, sides_ref, panel_ref, out_ref in zip(panels, sides_refs, panel_refs, out_refs):
        parts, width, shots = sides_ref.shape
        for part in range(parts):
            out_ref[part * width : (part + 1) * width] = inverse_ref[panel, part]
        start = parts * width
        out_ref[start : start + parts * shots] = transposed_sides(sides_ref).astype(jnp.bfloat16)
        start += parts * shots
        pieces = [(j, p) for j in range(panel_ref.shape[2] // width) for p in range(parts)]
        for n, (j, p) in enumerate(pieces):
            out_ref[start + n * width : start + (n + 1) * width] = panel_ref[p, :, j * width : (j + 1) * width]


def prepare(numbers, pivots, right_sides, panels, inverses):
    parts, local_rows, shots = right_sides.shape
    width = inverses.shape[-1]
    per_device = local_rows // width

    def slot(panel):
        return lambda i, pivots_ref: (0, lax.rem(pivots_ref[panel], per_device), 0)

    shapes = [(parts * (shots + (panel + 1) * width), width) for panel in numbers]
    return pl.pallas_call(
        functools.partial(prepare_kernel, numbers),
        out_shape=[jax.ShapeDtypeStruct(shape, jnp.bfloat16) for shape in shapes],
        grid_spec=pltpu.PrefetchScalarGridSpec(
            num_scalar_prefetch=1,
            grid=(1,),
            in_specs=[pl.BlockSpec(inverses.shape, lambda i, *_: (0, 0, 0, 0))]
            + [pl.BlockSpec((parts, width, shots), slot(panel)) for panel in numbers]
            + [pl.BlockSpec((parts, width, panel * width), slot(panel)) for panel in numbers],
            out_specs=[pl.BlockSpec(shape, lambda i, *_: (0, 0)) for shape in shapes],
        ),
        compiler_params=BESIDE_PANELS,
        name="prepare",
    )(pivots, inverses, *[right_sides] * len(numbers), *[panels] * len(numbers))


def solve_kernel(own_ref, *refs):
    solved_refs, out_ref = refs[:-1], refs[-1]
    height, width = out_ref.shape
    start = 2 * width + height
    rows = own_ref[2 * width : start].astype(jnp.float32)
    for solved_ref in solved_refs:
        solved = solved_ref[...]
        rows = rows - dot_t(solved, own_ref[start : start + width])
        rows = rows - dot_t(turned(solved), own_ref[start + width : start + 2 * width])
        start += 2 * width
    rows = rows.astype(jnp.bfloat16)
    solved = dot_t(rows, own_ref[:width]) + dot_t(turned(rows), own_ref[width : 2 * width])
    out_ref[...] = solved.astype(jnp.bfloat16)


def solve(own, solved):
    height, width = solved[0].shape
    return pl.pallas_call(
        solve_kernel,
        out_shape=jax.ShapeDtypeStruct((height, width), jnp.bfloat16),
        grid=(1,),
        in_specs=[pl.BlockSpec(own.shape, lambda i: (0, 0))]
        + [pl.BlockSpec(block.shape, lambda i: (0, 0)) for block in solved],
        out_specs=pl.BlockSpec((height, width), lambda i: (0, 0)),
        compiler_params=SMALL,
        name="solve",
    )(own, *solved)


def early_kernel(sides_ref, panel_ref, *refs):
    solved_refs, (out_ref, panel_out_ref, real_ref, imag_ref) = refs[:-4], refs[-4:]
    width = solved_refs[0].shape[1]

    @pl.when(pl.program_id(0) == 0)
    def _():
        for j, solved_ref in enumerate(solved_refs):
            solved = solved_ref[...]
            real_ref[:, j * width : (j + 1) * width] = solved
            imag_ref[:, j * width : (j + 1) * width] = turned(solved)

    columns = len(solved_refs) * width
    panel_out_ref[...] = panel_ref[:, :, columns:]
    values = transposed_sides(sides_ref) - dot_t(real_ref[...], panel_ref[0, :, :columns])
    out_ref[...] = values - dot_t(imag_ref[...], panel_ref[1, :, :columns])


def early_update(right_sides, panels, solved):
    parts, local_rows, shots = right_sides.shape
    height, width = solved[0].shape
    columns = len(solved) * width
    rest = panels.shape[2] - columns
    tile = TILES * width if local_rows % (TILES * width) == 0 else width
    return pl.pallas_call(
        early_kernel,
        out_shape=[
            jax.ShapeDtypeStruct((height, local_rows), jnp.float32),
            jax.ShapeDtypeStruct((parts, local_rows, rest), jnp.bfloat16),
        ],
        grid=(local_rows // tile,),
        in_specs=[
            pl.BlockSpec((parts, tile, shots), lambda i: (0, i, 0)),
            pl.BlockSpec((parts, tile, panels.shape[2]), lambda i: (0, i, 0)),
        ]
        + [pl.BlockSpec((height, width), lambda i: (0, 0)) for _ in solved],
        out_specs=[
            pl.BlockSpec((height, tile), lambda i: (0, i)),
            pl.BlockSpec((parts, tile, rest), lambda i: (0, i, 0)),
        ],
        scratch_shapes=[pltpu.VMEM((height, columns), jnp.bfloat16)] * 2,
        compiler_params=BESIDE_PANELS,
        name="early_update",
    )(right_sides, panels, *solved)


def last_kernel(panels, pivots_ref, me_ref, running_ref, panel_ref, *refs):
    width = panel_ref.shape[2]
    height, rows = running_ref.shape
    solved_refs, out_refs, whole_ref = refs[:panels], refs[panels:-1], refs[-1]
    count = len(out_refs)
    solved = solved_refs[-1][...]
    around = turned(solved)
    first = me_ref[0] * (rows // width)
    for k in range(rows // width):
        columns = slice(k * width, (k + 1) * width)
        values = running_ref[:, columns] - dot_t(solved, panel_ref[0, columns])
        whole_ref[:, columns] = (values - dot_t(around, panel_ref[1, columns])).astype(jnp.bfloat16)
    for j, solved_ref in enumerate(solved_refs):
        for k in range(rows // width):

            @pl.when(pivots_ref[j] == first + k)
            def _():
                whole_ref[:, k * width : (k + 1) * width] = solved_ref[...]

    each = height // 2 // count
    for step, out_ref in enumerate(out_refs):
        for part in range(2):
            start = pl.multiple_of((part * count + (me_ref[0] ^ step)) * each, each)
            out_ref[part] = whole_ref[pl.ds(start, each), :]


def last_update(me, pivots, running, panel, solved, owners):
    parts, local_rows, _ = panel.shape
    height, width = solved[0].shape
    each = height // parts // owners
    return pl.pallas_call(
        functools.partial(last_kernel, len(solved)),
        out_shape=[jax.ShapeDtypeStruct((parts, each, local_rows), jnp.bfloat16)] * owners,
        in_specs=[pl.BlockSpec(memory_space=pltpu.SMEM)] * 2
        + [pl.BlockSpec(memory_space=pltpu.VMEM)] * (2 + len(solved)),
        out_specs=[pl.BlockSpec(memory_space=pltpu.VMEM)] * owners,
        scratch_shapes=[pltpu.VMEM((height, local_rows), jnp.bfloat16)],
        compiler_params=SMALL,
        name="last_update",
    )(pivots, me, running, panel, *solved)


def regroup_kernel(me_ref, *refs):
    block_refs, out_ref, sems = refs[:-2], refs[-2], refs[-1]
    rows = block_refs[0].shape[2]
    copies = []
    for step, block_ref in enumerate(block_refs):
        start = pl.multiple_of((me_ref[0] ^ step) * rows, rows)
        copies.append(pltpu.make_async_copy(block_ref, out_ref.at[:, 0, :, pl.ds(start, rows)], sems.at[step]))
    for copy in copies:
        copy.start()
    for copy in copies:
        copy.wait()


def regroup(me, blocks):
    parts, shots, rows = blocks[0].shape
    return pl.pallas_call(
        regroup_kernel,
        out_shape=jax.ShapeDtypeStruct((parts, 1, shots, len(blocks) * rows), blocks[0].dtype),
        grid_spec=pltpu.PrefetchScalarGridSpec(
            num_scalar_prefetch=1,
            grid=(1,),
            in_specs=[pl.BlockSpec(memory_space=pltpu.VMEM)] * len(blocks),
            out_specs=pl.BlockSpec(memory_space=pl.ANY),
            scratch_shapes=[pltpu.SemaphoreType.DMA((len(blocks),))],
        ),
        compiler_params=SMALL,
        name="regroup",
    )(me, *blocks)


def broadcast(block, owner, beside):
    me = lax.axis_index("rows")

    def branch(source):
        def run(value):
            early = [lax.ppermute(value, "rows", [(source, source ^ step)]) for step in (7, 1, 4)]
            have = jnp.where(me == source, value, early[1] + early[2])
            results = beside()
            corner = [source ^ step for step in (0, 1, 4, 5)]
            fourth = lax.ppermute(have, "rows", [(source ^ 4, source ^ 5)])
            third = lax.ppermute(have, "rows", sorted((device, device ^ 2) for device in corner))
            return have + early[0] + third + fourth, results

        return run

    return lax.switch(owner, [branch(source) for source in range(RANKS)], block)


def solve_eight(right_sides, panels, inverses, pivots):
    last = inverses.shape[0] - 1
    block, *owners = solve_first(pivots, right_sides, inverses)
    owners = [owner[0] for owner in owners]
    block, own = broadcast(block, owners[0], lambda: prepare((1,), pivots, right_sides, panels, inverses))
    solved = [block]
    for panel in range(1, last):
        block = solve(own[-1], solved)
        block, more = broadcast(
            block, owners[panel], lambda: prepare((panel + 1,), pivots, right_sides, panels, inverses)
        )
        own = own + more
        solved.append(block)
    block = solve(own[last - 1], solved)
    block, (running, panel) = broadcast(block, owners[last], lambda: early_update(right_sides, panels, solved))
    solved.append(block)
    return solved, running, panel


def complex_dot(matrix, vectors):
    half = vectors.shape[0] // 2
    return dot_t(vectors, matrix[0]) + dot_t(turned(vectors), matrix[1])


def solve_summed(me, owners, right_sides, panels, inverses, pivots):
    parts, local_rows, shots = right_sides.shape
    width = inverses.shape[-1]
    solved = []
    for panel in range(inverses.shape[0]):
        offset = lax.rem(pivots[panel], local_rows // width) * width
        rows = lax.dynamic_slice_in_dim(right_sides, offset, width, 1)
        rows = jnp.transpose(rows, (0, 2, 1)).reshape(parts * shots, width).astype(jnp.float32)
        factor = lax.dynamic_slice_in_dim(panels, offset, width, 1)
        for j, block in enumerate(solved):
            rows = rows - complex_dot(factor[:, :, j * width : (j + 1) * width], block)
        block = complex_dot(inverses[panel], rows.astype(jnp.bfloat16)).astype(jnp.bfloat16)
        block = jnp.where(me == owners[panel], block, jnp.zeros_like(block))
        solved.append(lax.psum(block, "rows"))
    return solved


def body(ranks, right_sides, panels, inverses, pivots):
    me = lax.axis_index("rows")
    if ranks == RANKS:
        solved, running, panel = solve_eight(right_sides, panels, inverses, pivots)
    else:
        per_device = right_sides.shape[1] // inverses.shape[-1]
        owners = lax.div(pivots, jnp.full_like(pivots, per_device))
        solved = solve_summed(me, owners, right_sides, panels, inverses, pivots)
        running, panel = early_update(right_sides, panels, solved[:-1])
    me = me.reshape(1)
    blocks = list(last_update(me, pivots, running, panel, solved, ranks))
    for step in range(1, ranks):
        blocks[step] = lax.ppermute(blocks[step], "rows", [(i, i ^ step) for i in range(ranks)])
    return regroup(me, blocks)


def solution(mesh):
    placed = (
        P(None, "rows", ("groups", "shots")),
        P(None, ("groups", "rows"), None),
        P("groups", None, None, None),
        P(),
    )
    return jax.shard_map(
        functools.partial(body, mesh.shape["rows"]),
        mesh=mesh,
        in_specs=placed,
        out_specs=P(None, "shots", ("groups", "rows"), None),
        check_vma=False,
    )
```

```python
import functools

import jax
import jax.numpy as jnp
from jax import lax
from jax.experimental import pallas as pl
from jax.experimental.pallas import tpu as pltpu
from jax.sharding import PartitionSpec as P

CONTRACT_LAST = (((1,), (1,)), ((), ()))

BESIDE_PANELS = pltpu.CompilerParams(vmem_limit_bytes=52 * 1024 * 1024)
TILES = 4
RANKS = 8
SMALL = pltpu.CompilerParams(vmem_limit_bytes=16 * 1024 * 1024)


def dot_t(left, right):
    return lax.dot_general(left, right, CONTRACT_LAST, preferred_element_type=jnp.float32)


def turned(vectors):
    half = vectors.shape[0] // 2
    return jnp.concatenate([-vectors[half:], vectors[:half]], axis=0)


def transposed_sides(sides):
    shots = sides.shape[2]
    row = lax.broadcasted_iota(jnp.int32, (shots, shots), 0)
    column = lax.broadcasted_iota(jnp.int32, (shots, shots), 1)
    unit = jnp.where(row == column, 1.0, 0.0).astype(jnp.bfloat16)
    return jnp.concatenate([dot_t(unit, sides[0]), dot_t(unit, sides[1])], axis=0)


def first_kernel(per_device, pivots_ref, sides_ref, inverse_ref, out_ref, *owner_refs):
    for panel, owner_ref in enumerate(owner_refs):
        owner_ref[0] = lax.div(pivots_ref[panel], per_device)
    rows = transposed_sides(sides_ref).astype(jnp.bfloat16)
    solved = dot_t(rows, inverse_ref[0, 0]) + dot_t(turned(rows), inverse_ref[0, 1])
    out_ref[...] = solved.astype(jnp.bfloat16)


def solve_first(pivots, right_sides, inverses):
    parts, local_rows, shots = right_sides.shape
    count, width = inverses.shape[0], inverses.shape[-1]
    per_device = local_rows // width
    return pl.pallas_call(
        functools.partial(first_kernel, per_device),
        out_shape=[jax.ShapeDtypeStruct((parts * shots, width), jnp.bfloat16)]
        + [jax.ShapeDtypeStruct((1,), jnp.int32)] * count,
        grid_spec=pltpu.PrefetchScalarGridSpec(
            num_scalar_prefetch=1,
            grid=(1,),
            in_specs=[
                pl.BlockSpec((parts, width, shots), lambda i, p: (0, lax.rem(p[0], per_device), 0)),
                pl.BlockSpec((1, parts, width, width), lambda i, *_: (0, 0, 0, 0)),
            ],
            out_specs=[pl.BlockSpec((parts * shots, width), lambda i, *_: (0, 0))]
            + [pl.BlockSpec(memory_space=pltpu.SMEM)] * count,
        ),
        compiler_params=BESIDE_PANELS,
        name="solve_first",
    )(pivots, right_sides, inverses)


def prepare_kernel(panels, pivots_ref, inverse_ref, *refs):
    count = len(panels)
    sides_refs, panel_refs, out_refs = refs[:count], refs[count : 2 * count], refs[2 * count :]
    for panel, sides_ref, panel_ref, out_ref in zip(panels, sides_refs, panel_refs, out_refs):
        parts, width, shots = sides_ref.shape
        for part in range(parts):
            out_ref[part * width : (part + 1) * width] = inverse_ref[panel, part]
        start = parts * width
        out_ref[start : start + parts * shots] = transposed_sides(sides_ref).astype(jnp.bfloat16)
        start += parts * shots
        pieces = [(j, p) for j in range(panel_ref.shape[2] // width) for p in range(parts)]
        for n, (j, p) in enumerate(pieces):
            out_ref[start + n * width : start + (n + 1) * width] = panel_ref[p, :, j * width : (j + 1) * width]


def prepare(numbers, pivots, right_sides, panels, inverses):
    parts, local_rows, shots = right_sides.shape
    width = inverses.shape[-1]
    per_device = local_rows // width

    def slot(panel):
        return lambda i, pivots_ref: (0, lax.rem(pivots_ref[panel], per_device), 0)

    shapes = [(parts * (shots + (panel + 1) * width), width) for panel in numbers]
    return pl.pallas_call(
        functools.partial(prepare_kernel, numbers),
        out_shape=[jax.ShapeDtypeStruct(shape, jnp.bfloat16) for shape in shapes],
        grid_spec=pltpu.PrefetchScalarGridSpec(
            num_scalar_prefetch=1,
            grid=(1,),
            in_specs=[pl.BlockSpec(inverses.shape, lambda i, *_: (0, 0, 0, 0))]
            + [pl.BlockSpec((parts, width, shots), slot(panel)) for panel in numbers]
            + [pl.BlockSpec((parts, width, panel * width), slot(panel)) for panel in numbers],
            out_specs=[pl.BlockSpec(shape, lambda i, *_: (0, 0)) for shape in shapes],
        ),
        compiler_params=BESIDE_PANELS,
        name="prepare",
    )(pivots, inverses, *[right_sides] * len(numbers), *[panels] * len(numbers))


def solve_kernel(own_ref, *refs):
    solved_refs, out_ref = refs[:-1], refs[-1]
    height, width = out_ref.shape
    start = 2 * width + height
    rows = own_ref[2 * width : start].astype(jnp.float32)
    for solved_ref in solved_refs:
        solved = solved_ref[...]
        rows = rows - dot_t(solved, own_ref[start : start + width])
        rows = rows - dot_t(turned(solved), own_ref[start + width : start + 2 * width])
        start += 2 * width
    rows = rows.astype(jnp.bfloat16)
    solved = dot_t(rows, own_ref[:width]) + dot_t(turned(rows), own_ref[width : 2 * width])
    out_ref[...] = solved.astype(jnp.bfloat16)


def solve(own, solved):
    height, width = solved[0].shape
    return pl.pallas_call(
        solve_kernel,
        out_shape=jax.ShapeDtypeStruct((height, width), jnp.bfloat16),
        grid=(1,),
        in_specs=[pl.BlockSpec(own.shape, lambda i: (0, 0))]
        + [pl.BlockSpec(block.shape, lambda i: (0, 0)) for block in solved],
        out_specs=pl.BlockSpec((height, width), lambda i: (0, 0)),
        compiler_params=SMALL,
        name="solve",
    )(own, *solved)


def early_kernel(sides_ref, panel_ref, *refs):
    solved_refs, (out_ref, panel_out_ref, real_ref, imag_ref) = refs[:-4], refs[-4:]
    width = solved_refs[0].shape[1]

    @pl.when(pl.program_id(0) == 0)
    def _():
        for j, solved_ref in enumerate(solved_refs):
            solved = solved_ref[...]
            real_ref[:, j * width : (j + 1) * width] = solved
            imag_ref[:, j * width : (j + 1) * width] = turned(solved)

    columns = len(solved_refs) * width
    panel_out_ref[...] = panel_ref[:, :, columns:]
    values = transposed_sides(sides_ref) - dot_t(real_ref[...], panel_ref[0, :, :columns])
    out_ref[...] = values - dot_t(imag_ref[...], panel_ref[1, :, :columns])


def early_update(right_sides, panels, solved):
    parts, local_rows, shots = right_sides.shape
    height, width = solved[0].shape
    columns = len(solved) * width
    rest = panels.shape[2] - columns
    tile = TILES * width if local_rows % (TILES * width) == 0 else width
    return pl.pallas_call(
        early_kernel,
        out_shape=[
            jax.ShapeDtypeStruct((height, local_rows), jnp.float32),
            jax.ShapeDtypeStruct((parts, local_rows, rest), jnp.bfloat16),
        ],
        grid=(local_rows // tile,),
        in_specs=[
            pl.BlockSpec((parts, tile, shots), lambda i: (0, i, 0)),
            pl.BlockSpec((parts, tile, panels.shape[2]), lambda i: (0, i, 0)),
        ]
        + [pl.BlockSpec((height, width), lambda i: (0, 0)) for _ in solved],
        out_specs=[
            pl.BlockSpec((height, tile), lambda i: (0, i)),
            pl.BlockSpec((parts, tile, rest), lambda i: (0, i, 0)),
        ],
        scratch_shapes=[pltpu.VMEM((height, columns), jnp.bfloat16)] * 2,
        compiler_params=BESIDE_PANELS,
        name="early_update",
    )(right_sides, panels, *solved)


def last_kernel(panels, pivots_ref, me_ref, running_ref, panel_ref, *refs):
    width = panel_ref.shape[2]
    height, rows = running_ref.shape
    solved_refs, out_refs, whole_ref = refs[:panels], refs[panels:-1], refs[-1]
    count = len(out_refs)
    solved = solved_refs[-1][...]
    around = turned(solved)
    first = me_ref[0] * (rows // width)
    for k in range(rows // width):
        columns = slice(k * width, (k + 1) * width)
        values = running_ref[:, columns] - dot_t(solved, panel_ref[0, columns])
        whole_ref[:, columns] = (values - dot_t(around, panel_ref[1, columns])).astype(jnp.bfloat16)
    for j, solved_ref in enumerate(solved_refs):
        for k in range(rows // width):

            @pl.when(pivots_ref[j] == first + k)
            def _():
                whole_ref[:, k * width : (k + 1) * width] = solved_ref[...]

    each = height // 2 // count
    for step, out_ref in enumerate(out_refs):
        for part in range(2):
            start = pl.multiple_of((part * count + (me_ref[0] ^ step)) * each, each)
            out_ref[part] = whole_ref[pl.ds(start, each), :]


def last_update(me, pivots, running, panel, solved, owners):
    parts, local_rows, _ = panel.shape
    height, width = solved[0].shape
    each = height // parts // owners
    return pl.pallas_call(
        functools.partial(last_kernel, len(solved)),
        out_shape=[jax.ShapeDtypeStruct((parts, each, local_rows), jnp.bfloat16)] * owners,
        in_specs=[pl.BlockSpec(memory_space=pltpu.SMEM)] * 2
        + [pl.BlockSpec(memory_space=pltpu.VMEM)] * (2 + len(solved)),
        out_specs=[pl.BlockSpec(memory_space=pltpu.VMEM)] * owners,
        scratch_shapes=[pltpu.VMEM((height, local_rows), jnp.bfloat16)],
        compiler_params=SMALL,
        name="last_update",
    )(pivots, me, running, panel, *solved)


def regroup_kernel(me_ref, *refs):
    block_refs, out_ref, sems = refs[:-2], refs[-2], refs[-1]
    rows = block_refs[0].shape[2]
    copies = []
    for step, block_ref in enumerate(block_refs):
        start = pl.multiple_of((me_ref[0] ^ step) * rows, rows)
        copies.append(pltpu.make_async_copy(block_ref, out_ref.at[:, 0, :, pl.ds(start, rows)], sems.at[step]))
    for copy in copies:
        copy.start()
    for copy in copies:
        copy.wait()


def regroup(me, blocks):
    parts, shots, rows = blocks[0].shape
    return pl.pallas_call(
        regroup_kernel,
        out_shape=jax.ShapeDtypeStruct((parts, 1, shots, len(blocks) * rows), blocks[0].dtype),
        grid_spec=pltpu.PrefetchScalarGridSpec(
            num_scalar_prefetch=1,
            grid=(1,),
            in_specs=[pl.BlockSpec(memory_space=pltpu.VMEM)] * len(blocks),
            out_specs=pl.BlockSpec(memory_space=pl.ANY),
            scratch_shapes=[pltpu.SemaphoreType.DMA((len(blocks),))],
        ),
        compiler_params=SMALL,
        name="regroup",
    )(me, *blocks)


def broadcast(block, owner, beside):
    me = lax.axis_index("rows")

    def branch(source):
        def run(value):
            early = [lax.ppermute(value, "rows", [(source, source ^ step)]) for step in (7, 1, 4)]
            have = jnp.where(me == source, value, early[1] + early[2])
            results = beside()
            corner = [source ^ step for step in (0, 1, 4, 5)]
            fourth = lax.ppermute(have, "rows", [(source ^ 4, source ^ 5)])
            third = lax.ppermute(have, "rows", sorted((device, device ^ 2) for device in corner))
            return have + early[0] + third + fourth, results

        return run

    return lax.switch(owner, [branch(source) for source in range(RANKS)], block)


def solve_eight(right_sides, panels, inverses, pivots):
    last = inverses.shape[0] - 1
    block, *owners = solve_first(pivots, right_sides, inverses)
    owners = [owner[0] for owner in owners]
    block, own = broadcast(block, owners[0], lambda: prepare((1,), pivots, right_sides, panels, inverses))
    solved = [block]
    for panel in range(1, last):
        block = solve(own[-1], solved)
        block, more = broadcast(
            block, owners[panel], lambda: prepare((panel + 1,), pivots, right_sides, panels, inverses)
        )
        own = own + more
        solved.append(block)
    block = solve(own[last - 1], solved)
    block, (running, panel) = broadcast(block, owners[last], lambda: early_update(right_sides, panels, solved))
    solved.append(block)
    return solved, running, panel


def complex_dot(matrix, vectors):
    half = vectors.shape[0] // 2
    return dot_t(vectors, matrix[0]) + dot_t(turned(vectors), matrix[1])


def solve_summed(me, owners, right_sides, panels, inverses, pivots):
    parts, local_rows, shots = right_sides.shape
    width = inverses.shape[-1]
    solved = []
    for panel in range(inverses.shape[0]):
        offset = lax.rem(pivots[panel], local_rows // width) * width
        rows = lax.dynamic_slice_in_dim(right_sides, offset, width, 1)
        rows = jnp.transpose(rows, (0, 2, 1)).reshape(parts * shots, width).astype(jnp.float32)
        factor = lax.dynamic_slice_in_dim(panels, offset, width, 1)
        for j, block in enumerate(solved):
            rows = rows - complex_dot(factor[:, :, j * width : (j + 1) * width], block)
        block = complex_dot(inverses[panel], rows.astype(jnp.bfloat16)).astype(jnp.bfloat16)
        block = jnp.where(me == owners[panel], block, jnp.zeros_like(block))
        solved.append(lax.psum(block, "rows"))
    return solved


def body(ranks, right_sides, panels, inverses, pivots):
    me = lax.axis_index("rows")
    if ranks == RANKS:
        solved, running, panel = solve_eight(right_sides, panels, inverses, pivots)
    else:
        per_device = right_sides.shape[1] // inverses.shape[-1]
        owners = lax.div(pivots, jnp.full_like(pivots, per_device))
        solved = solve_summed(me, owners, right_sides, panels, inverses, pivots)
        running, panel = early_update(right_sides, panels, solved[:-1])
    me = me.reshape(1)
    blocks = list(last_update(me, pivots, running, panel, solved, ranks))
    for step in range(1, ranks):
        blocks[step] = lax.ppermute(blocks[step], "rows", [(i, i ^ step) for i in range(ranks)])
    return regroup(me, blocks)


def solution(mesh):
    placed = (
        P(None, "rows", ("groups", "shots")),
        P(None, ("groups", "rows"), None),
        P("groups", None, None, None),
        P(),
    )
    return jax.shard_map(
        functools.partial(body, mesh.shape["rows"]),
        mesh=mesh,
        in_specs=placed,
        out_specs=P(None, "shots", ("groups", "rows"), None),
        check_vma=False,
    )
```
